256 devices in a mesh: dp: 32 (over x, z_lo, y), tensor: 8 (over z_hi, core).
Axes of the slice: x: 4, y: 4, z: 8 (z_hi: 4, z_lo: 2; z = z_hi * 2 + z_lo), core: 2. Of those that a mesh axis runs over, the one named last changes fastest.
Arguments:
- enc_states: bfloat16 [4096, 8192], P('dp'), may hold values from -170 to 170
- kv_cotangent: bfloat16 [4096, 2048], P('dp', 'tensor'), may hold values from -120 to 120
- out_cotangent: bfloat16 [4096, 8192], P('dp'), may hold values from -400 to 400
- attn_context: bfloat16 [4096, 4096], P('dp', 'tensor'), may hold values from -35 to 35
- next_states: bfloat16 [4096, 8192], P('dp'), may hold values from -6 to 6
- next_context: bfloat16 [4096, 4096], P('dp', 'tensor'), may hold values from -6 to 6
- kv_master: float32 [8192, 2048], P('dp', 'tensor'), may hold values from -0.0625 to 0.0625
- kv_first: float32 [8192, 2048], P('dp', 'tensor'), may hold values from -0.6 to 0.6
- kv_second: float32 [8192, 2048], P('dp', 'tensor'), may hold values from 0.01 to 0.2
- out_master: float32 [8192, 4096], P('dp', 'tensor'), may hold values from -0.09375 to 0.09375
- out_first: float32 [8192, 4096], P('dp', 'tensor'), may hold values from -0.6 to 0.6
- out_second: float32 [8192, 4096], P('dp', 'tensor'), may hold values from 0.01 to 0.2
Outputs:
- new_kv_master: float32 [8192, 2048], P('dp', 'tensor')
- new_kv_first: float32 [8192, 2048], P('dp', 'tensor')
- new_kv_second: float32 [8192, 2048], P('dp', 'tensor')
- new_out_master: float32 [8192, 4096], P('dp', 'tensor')
- new_out_first: float32 [8192, 4096], P('dp', 'tensor')
- new_out_second: float32 [8192, 4096], P('dp', 'tensor')
- next_keyvalue: bfloat16 [4096, 2048], P('dp', 'tensor')
- next_output: bfloat16 [4096, 8192], P('dp', 'tensor')
The draws below stay inside these ranges and needn't reach their ends.
All inputs are finite; a program needn't handle non-finite values.
Results may differ from the reference program's by a relative error of at most 0.025.
Values may be sent and summed in bfloat16 or wider, within the bound.
No kernel may reach another device: no remote copies, remote signals or barrier semaphores. Data moves between devices by JAX's collectives and lax.ppermute only.
A program may use at most 128 MiB of HBM per device.

```python
import math
import jax
import jax.numpy as jnp
from jax import lax

D = 8192
TOK_DEV = 128
STEP = 10
TOKENS = 4096
KVW = 2048
QD = 4096
N_DP = 32
N_TENSOR = 8


def column_scales(key, extent, incline):
    spread = jax.random.uniform(key, (extent,), jnp.float32, -1.15, 1.15)
    position = jnp.arange(extent, dtype=jnp.float32) / extent - 0.5
    return jnp.exp(spread + 0.5 * math.log(incline) * position)


def spike_factor(key, row_count, column_count):
    row_block = jnp.arange(row_count) // (row_count // N_DP)
    column_block = jnp.arange(column_count) // (column_count // N_DP)
    paired = jax.random.permutation(key, N_DP)
    return jnp.where(paired[row_block][:, None] == column_block[None, :], 5.0, 1.0)


def token_signs(key, salt):
    picks = jax.random.randint(jax.random.fold_in(key, salt), (TOKENS,), 0, 2)
    return 2.0 * picks.astype(jnp.float32) - 1.0


def shared_part(key, signs, extent, scales):
    along = jnp.clip(jax.random.normal(key, (extent,), jnp.float32), -4.0, 4.0)
    amplitude = (2.6 / TOKENS) ** 0.25
    return amplitude * signs[:, None] * (along * scales)[None, :]


def draw_enc_states(key, part):
    signs = token_signs(key, 501)
    key = jax.random.fold_in(key, 11)
    noise_key = jax.random.fold_in(key, 0)
    scale_key = jax.random.fold_in(key, 1)
    spike_key = jax.random.fold_in(key, 2)
    along_key = jax.random.fold_in(key, 4)
    sample = jnp.clip(jax.random.normal(noise_key, (TOKENS, D), jnp.float32), -6.0, 6.0)
    scales = column_scales(scale_key, D, 3.0)
    values = sample * scales[None, :] * spike_factor(spike_key, TOKENS, D)
    values = values + shared_part(along_key, signs, D, scales)
    return values.astype(jnp.bfloat16)


def draw_kv_cotangent(key, part):
    signs = token_signs(key, 501)
    key = jax.random.fold_in(key, 23)
    noise_key = jax.random.fold_in(key, 0)
    scale_key = jax.random.fold_in(key, 1)
    along_key = jax.random.fold_in(key, 3)
    sample = jnp.clip(jax.random.normal(noise_key, (TOKENS, KVW), jnp.float32), -6.0, 6.0)
    scales = column_scales(scale_key, KVW, 3.0)
    values = sample * scales[None, :] + shared_part(along_key, signs, KVW, scales)
    return (values * math.sqrt(D / TOKENS)).astype(jnp.bfloat16)


def draw_out_cotangent(key, part):
    signs = token_signs(key, 733)
    key = jax.random.fold_in(key, 37)
    noise_key = jax.random.fold_in(key, 0)
    scale_key = jax.random.fold_in(key, 1)
    spike_key = jax.random.fold_in(key, 2)
    along_key = jax.random.fold_in(key, 4)
    sample = jnp.clip(jax.random.normal(noise_key, (TOKENS, D), jnp.float32), -6.0, 6.0)
    scales = column_scales(scale_key, D, 3.0)
    values = sample * scales[None, :] * spike_factor(spike_key, TOKENS, D)
    values = values + shared_part(along_key, signs, D, scales)
    return values.astype(jnp.bfloat16)


def draw_attn_context(key, part):
    signs = token_signs(key, 733)
    key = jax.random.fold_in(key, 41)
    noise_key = jax.random.fold_in(key, 0)
    scale_key = jax.random.fold_in(key, 1)
    along_key = jax.random.fold_in(key, 3)
    sample = jnp.clip(jax.random.normal(noise_key, (TOKENS, QD), jnp.float32), -6.0, 6.0)
    scales = column_scales(scale_key, QD, 3.0)
    values = sample * scales[None, :] + shared_part(along_key, signs, QD, scales)
    return values.astype(jnp.bfloat16)


def level_of(rng, dims, shards, least, top_value):
    level = 1.0
    for axis_at, parts in shards:
        draws = jax.random.uniform(jax.random.fold_in(jax.random.fold_in(rng, 6), axis_at), (parts,), jnp.float32, least / len(shards), top_value / len(shards))
        level = level * jnp.repeat(jnp.exp(draws), dims[axis_at] // parts).reshape((-1,) + (1,) * (len(dims) - 1 - axis_at))
    return level


def noise(rng, dims, scale, most, shards=(), held_as=jnp.bfloat16):
    loudness = level_of(rng, dims, shards, -0.22, 0.18) if shards else 1.0
    drawn = jax.random.normal(rng, dims, jnp.float32) * scale * loudness
    return jnp.minimum(jnp.maximum(drawn, -most), most).astype(held_as)


def setup_inputs(seed: int = 0) -> dict:
    key_of = jax.random.split(jax.random.key(seed), 13)
    enc_states = draw_enc_states(jax.random.fold_in(key_of[12], 71), 0)
    kv_cotangent = draw_kv_cotangent(jax.random.fold_in(key_of[12], 71), 0)
    out_cotangent = draw_out_cotangent(jax.random.fold_in(key_of[12], 71), 0)
    attn_context = draw_attn_context(jax.random.fold_in(key_of[12], 71), 0)
    next_states = noise(key_of[4], (TOKENS, D), 1.0, 6.0, ((0, 32),))
    next_context = noise(key_of[5], (TOKENS, QD), 1.0, 6.0, ((0, 32), (1, 8)))
    kv_master = noise(key_of[6], (D, KVW), D ** -0.5, 0.0625, ((0, 32), (1, 8)), jnp.float32)
    kv_first = noise(key_of[7], (D, KVW), 0.1, 0.6, ((0, 32), (1, 8)), jnp.float32)
    kv_second = jnp.clip(jnp.exp(math.log(0.2) - 2.9957323 * jax.random.uniform(key_of[8], (D, KVW), jnp.float32) ** level_of(key_of[8], (D, KVW), ((0, 32), (1, 8)), -0.2, 0.2)), 0.01, 0.2)
    out_master = noise(key_of[9], (D, QD), QD ** -0.5, 0.09375, ((0, 32), (1, 8)), jnp.float32)
    out_first = noise(key_of[10], (D, QD), 0.1, 0.6, ((0, 32), (1, 8)), jnp.float32)
    out_second = jnp.clip(jnp.exp(math.log(0.2) - 2.9957323 * jax.random.uniform(key_of[11], (D, QD), jnp.float32) ** level_of(key_of[11], (D, QD), ((0, 32), (1, 8)), -0.2, 0.2)), 0.01, 0.2)
    return dict(enc_states=enc_states, kv_cotangent=kv_cotangent, out_cotangent=out_cotangent, attn_context=attn_context, next_states=next_states, next_context=next_context, kv_master=kv_master, kv_first=kv_first, kv_second=kv_second, out_master=out_master, out_first=out_first, out_second=out_second)


beta_one = 0.9
beta_two = 0.95
learn_rate = 0.01
weight_decay = 0.1
epsilon = 1e-08
clip_ratio = 0.25

def adam_update(master, first_moment, second_moment, gradient, factor):
    scaled = gradient * factor
    first_moment = beta_one * first_moment + (1.0 - beta_one) * scaled
    second_moment = beta_two * second_moment + (1.0 - beta_two) * scaled * scaled
    first_hat = first_moment / (1.0 - beta_one ** STEP)
    second_hat = second_moment / (1.0 - beta_two ** STEP)
    direction = first_hat / (jnp.sqrt(second_hat) + epsilon)
    master = master - learn_rate * (direction + weight_decay * master)
    return (master, first_moment, second_moment)

def rounded(values):
    return lax.optimization_barrier(values.astype(jnp.bfloat16)).astype(jnp.float32)

def reference(enc_states, kv_cotangent, out_cotangent, attn_context, next_states, next_context, kv_master, kv_first, kv_second, out_master, out_first, out_second):
    kv_scale = D ** (-0.5)
    out_scale = QD ** (-0.5)
    groups = (enc_states.reshape(N_DP, TOK_DEV, D), kv_cotangent.reshape(N_DP, TOK_DEV, KVW), out_cotangent.reshape(N_DP, TOK_DEV, D), attn_context.reshape(N_DP, TOK_DEV, QD))

    def accumulate(running, blocks):
        states, kv_cot, out_cot, context = blocks
        kv_term = jnp.dot(states.T, kv_cot, preferred_element_type=jnp.float32) * kv_scale
        out_term = jnp.dot(out_cot.T, context, preferred_element_type=jnp.float32) * out_scale
        return ((running[0] + rounded(kv_term), running[1] + rounded(out_term)), None)
    start_sums = (jnp.zeros((D, KVW), jnp.float32), jnp.zeros((D, QD), jnp.float32))
    (kv_grad, out_grad), unused = lax.scan(accumulate, start_sums, groups)
    squares_total = jnp.sum(kv_grad * kv_grad) + jnp.sum(out_grad * out_grad)
    max_norm = clip_ratio * (D * (KVW + QD)) ** 0.5
    factor = jnp.minimum(1.0, max_norm / (jnp.sqrt(squares_total) + 1e-06))
    new_kv_master, new_kv_first, new_kv_second = adam_update(kv_master, kv_first, kv_second, kv_grad, factor)
    new_out_master, new_out_first, new_out_second = adam_update(out_master, out_first, out_second, out_grad, factor)
    kv_weight = new_kv_master.astype(jnp.bfloat16)
    out_weight = new_out_master.astype(jnp.bfloat16)
    next_keyvalue = jnp.dot(next_states, kv_weight, preferred_element_type=jnp.float32).astype(jnp.bfloat16)
    group_width = QD // N_TENSOR
    context_groups = jnp.moveaxis(next_context.reshape(TOKENS, N_TENSOR, group_width), 1, 0)
    weight_groups = jnp.moveaxis(out_weight.reshape(D, N_TENSOR, group_width), 1, 0)

    def add_group(running, blocks):
        context, weights = blocks
        partial_out = jnp.dot(context, weights.T, preferred_element_type=jnp.float32)
        return (running + rounded(partial_out), None)
    summed, unused = lax.scan(add_group, jnp.zeros((TOKENS, D), jnp.float32), (context_groups, weight_groups))
    next_output = summed.astype(jnp.bfloat16)
    return (new_kv_master, new_kv_first, new_kv_second, new_out_master, new_out_first, new_out_second, next_keyvalue, next_output)
```

```python
import itertools
import math

import jax
import jax.numpy as jnp
from jax import lax
from jax.experimental import pallas as pl
from jax.experimental.pallas import tpu as pltpu
from jax.sharding import PartitionSpec as P

D = 8192
STEP = 10
KVW = 2048
QD = 4096

NX, NZ, NY = 4, 2, 4
NH, NC = 4, 2
TOK = 128
HALF = TOK // 2
ROWS = 256
WIDE = NX * ROWS

beta_one = 0.9
beta_two = 0.95
learn_rate = 0.01
weight_decay = 0.1
epsilon = 1e-08
clip_ratio = 0.25


def dp_of(x, z, y):
    return (x * NZ + z) * NY + y


ZY_GROUPS = [[dp_of(x, z, y) for z in range(NZ) for y in range(NY)] for x in range(NX)]


def device_pairs(target):
    pairs = []
    for x, z, y, h, c in itertools.product(
        range(NX), range(NZ), range(NY), range(NH), range(NC)
    ):
        tx, tz, ty, th, tc = target(x, z, y, h, c)
        source = (dp_of(x, z, y) * NH + h) * NC + c
        pairs.append((source, (dp_of(tx % NX, tz % NZ, ty % NY) * NH + th % NH) * NC + tc % NC))
    return pairs


def move(values, target):
    return lax.ppermute(values, ("dp", "tensor"), device_pairs(target))


def move_core(values):
    return move(values, lambda x, z, y, h, c: (x, z, y, h, c + 1))


def move_x(values, k):
    return move(values, lambda x, z, y, h, c: (x + k, z, y, h, c))


def move_y(values, k):
    return move(values, lambda x, z, y, h, c: (x, z, y + k, h, c))


def move_h(values, k):
    return move(values, lambda x, z, y, h, c: (x, z, y, h + k, c))


def move_z(values):
    return move(values, lambda x, z, y, h, c: (x, z + 1, y, h, c))


def swap_xh(values):
    return move(values, lambda x, z, y, h, c: (h, z, y, x, c))


def move_home(values, k):
    return move(values, lambda x, z, y, h, c: (x + k, c, y, h, z))


def adam_update(master, first_moment, second_moment, gradient, factor):
    scaled = gradient * factor
    first_moment = beta_one * first_moment + (1.0 - beta_one) * scaled
    second_moment = beta_two * second_moment + (1.0 - beta_two) * scaled * scaled
    first_hat = first_moment / (1.0 - beta_one**STEP)
    second_hat = second_moment / (1.0 - beta_two**STEP)
    direction = first_hat / (jnp.sqrt(second_hat) + epsilon)
    master = master - learn_rate * (direction + weight_decay * master)
    return (master, first_moment, second_moment)


def dot(left, right, left_dims, right_dims):
    return lax.dot_general(
        left,
        right,
        ((left_dims, right_dims), ((), ())),
        preferred_element_type=jnp.float32,
    )


VMEM = pl.BlockSpec(memory_space=pltpu.VMEM)
SMEM = pl.BlockSpec(memory_space=pltpu.SMEM)


def call(kernel, out_shape, operands, scalars=(), flops=0, scratch=()):
    moved = sum(o.size * o.dtype.itemsize for o in (*operands, *jax.tree.leaves(out_shape)))
    return pl.pallas_call(
        kernel,
        out_shape=out_shape,
        in_specs=[SMEM] * len(scalars) + [VMEM] * len(operands),
        out_specs=jax.tree.map(lambda _: VMEM, out_shape),
        scratch_shapes=list(scratch),
        compiler_params=pltpu.CompilerParams(vmem_limit_bytes=40 * 2**20),
        cost_estimate=pl.CostEstimate(flops=flops, bytes_accessed=moved, transcendentals=0),
    )(*scalars, *operands)


def shape(dims, dtype=jnp.bfloat16):
    return jax.ShapeDtypeStruct(dims, dtype)


def contract(left, right, left_dim, right_dim):
    return lax.dot_general(
        left, right, (((left_dim,), (right_dim,)), ((), ())), preferred_element_type=jnp.float32
    )


def halves(core):
    own = pl.ds(pl.multiple_of(core * HALF, HALF), HALF)
    other = pl.ds(pl.multiple_of((1 - core) * HALF, HALF), HALF)
    return own, other


def columns_of(x, k, p=None):
    first = lax.rem(x + k, NX) * (NZ * NY)
    if p is None:
        return pl.ds(pl.multiple_of(first * ROWS, ROWS), NZ * NY * ROWS)
    return pl.ds(pl.multiple_of((first + p) * ROWS, ROWS), ROWS)


def kv_payload(place, enc_states, kv_cotangent):
    width = NZ * NY * ROWS
    kvw = kv_cotangent.shape[1]

    def kernel(place_ref, states_ref, cot_ref, o0, o1, o2, o3, rest_ref):
        x, core = place_ref[0], place_ref[4]
        own, other = halves(core)
        for k, out_ref in enumerate((o0, o1, o2, o3)):
            out_ref[:, :width] = states_ref[own, columns_of(x, k)]
            out_ref[:, width : width + kvw] = cot_ref[own, :]
            out_ref[:, width + kvw :] = cot_ref[other, :]
        rest_ref[...] = states_ref[other, columns_of(x, 0)]

    out_shape = (shape((HALF, width + 2 * kvw)),) * NX + (shape((HALF, width)),)
    return call(kernel, out_shape, (enc_states, kv_cotangent), (place,))


def out_payload(place, out_cotangent, attn_context):
    qd = attn_context.shape[1]

    def kernel(place_ref, cot_ref, context_ref, out_ref):
        x, core = place_ref[0], place_ref[4]
        own, other = halves(core)
        for p in range(NZ * NY):
            for k in range(NX):
                rows = slice((k // 2) * HALF, (k // 2 + 1) * HALF)
                cols = slice((k % 2) * ROWS, (k % 2 + 1) * ROWS)
                out_ref[p, rows, cols] = cot_ref[own, columns_of(x, k, p)]
            out_ref[p, :HALF, 2 * ROWS :] = context_ref[own, :]
            out_ref[p, HALF:, 2 * ROWS :] = context_ref[other, :]

    out_shape = shape((NZ * NY, TOK, 2 * ROWS + qd))
    return call(kernel, out_shape, (out_cotangent, attn_context), (place,))


def kv_terms(place, own, other, next_states, kvw, scale):
    width = NZ * NY * ROWS

    def kernel(place_ref, *refs):
        own_refs, other_refs, states_ref, out_ref = (
            refs[:NX],
            refs[NX : 2 * NX],
            refs[2 * NX],
            refs[2 * NX + 1],
        )
        x, core = place_ref[0], place_ref[4]
        half, _ = halves(core)
        own_cot = jnp.concatenate([r[:, width : width + kvw] for r in own_refs], axis=0)
        other_cot = jnp.concatenate([r[:, width + kvw :] for r in own_refs], axis=0)
        for p in range(NZ * NY):
            cols = slice(p * ROWS, (p + 1) * ROWS)
            term = contract(own_cot, jnp.concatenate([r[:, cols] for r in own_refs]), 0, 0)
            term += contract(other_cot, jnp.concatenate([r[:, cols] for r in other_refs]), 0, 0)
            out_ref[p, :kvw] = (term * scale).astype(jnp.bfloat16)
            for k in range(NX):
                rows = slice(kvw + k * HALF, kvw + (k + 1) * HALF)
                out_ref[p, rows] = states_ref[half, columns_of(x, k, p)]

    out_shape = shape((NZ * NY, kvw + NX * HALF, ROWS))
    return call(kernel, out_shape, (*own, *other, next_states), (place,), flops=2**29)


def out_terms(own, other, qd, scale):
    tokens = NZ * NY * HALF

    def kernel(own_ref, other_ref, *out_refs):
        own_context = own_ref[:, :HALF, 2 * ROWS :].reshape(tokens, qd)
        other_context = own_ref[:, HALF:, 2 * ROWS :].reshape(tokens, qd)
        for k, out_ref in enumerate(out_refs):
            rows = slice((k // 2) * HALF, (k // 2 + 1) * HALF)
            cols = slice((k % 2) * ROWS, (k % 2 + 1) * ROWS)
            term = contract(own_context, own_ref[:, rows, cols].reshape(tokens, ROWS), 0, 0)
            term += contract(other_context, other_ref[:, rows, cols].reshape(tokens, ROWS), 0, 0)
            out_ref[...] = (term * scale).astype(jnp.bfloat16)

    return call(kernel, (shape((qd, ROWS)),) * NX, (own, other), flops=2**30)


def sum_terms(terms, columns):
    rows = terms[0].shape[-1]

    def kernel(*refs):
        *term_refs, grad_ref, squares_ref = refs
        total = None
        for ref in term_refs:
            parts = [ref[...]] if len(ref.shape) == 2 else [ref[i, :columns] for i in range(ref.shape[0])]
            for part in parts:
                part = part.astype(jnp.float32)
                total = part if total is None else total + part
        squares_ref[0, 0] = jnp.sum(total * total)
        grad_ref[...] = total.T

    return pl.pallas_call(
        kernel,
        out_shape=(shape((rows, columns), jnp.float32), shape((1, 1), jnp.float32)),
        in_specs=[VMEM] * len(terms),
        out_specs=(VMEM, SMEM),
        compiler_params=pltpu.CompilerParams(vmem_limit_bytes=40 * 2**20),
        cost_estimate=pl.CostEstimate(flops=2**20, bytes_accessed=2**20, transcendentals=0),
    )(*terms)


def next_partial(place, which, context, weights, arrived=None):
    qd = context[0].shape[-1]
    n_in = NH + NY

    def kernel(place_ref, which_ref, *refs):
        x, y, h = place_ref[0], place_ref[2], place_ref[3]
        *refs, tokens_ref = refs
        outs = refs[n_in + (arrived is not None) :]
        for j in range(NH):
            tokens_ref[lax.rem(h - j - x + 2 * NX, NX)] = refs[j][which_ref[0]]
        tokens = tokens_ref[...].reshape(NX * TOK, qd)
        for j in range(NY):
            cols = pl.ds(pl.multiple_of(lax.rem(y - j + NY, NY) * ROWS, ROWS), ROWS)
            part = contract(tokens, refs[NH + j][...], 1, 1)
            if arrived is None:
                outs[0][:, cols] = part.astype(jnp.bfloat16)
            else:
                part += refs[n_in][:, cols].astype(jnp.float32)
                for k in range(NX):
                    outs[k][:, cols] = part[k * TOK : (k + 1) * TOK].astype(jnp.bfloat16)

    if arrived is None:
        out_shape = (shape((NX * TOK, NY * ROWS)),)
        operands = (*context, *weights)
    else:
        out_shape = (shape((TOK, NY * ROWS)),) * NX
        operands = (*context, *weights, arrived)
    scratch = [pltpu.VMEM((NX, TOK, qd), jnp.bfloat16)]
    return call(kernel, out_shape, operands, (place, which), 2**29, scratch)


def keyvalue_partial(own, other, weights):
    kvw = weights[0].shape[1]

    def kernel(own_ref, other_ref, w0, w1, w2, w3, out_ref):
        for half, ref in enumerate((own_ref, other_ref)):
            total = None
            for j, weight in enumerate((w0, w1, w2, w3)):
                first = ref.shape[1] - (NX - -j % NX) * HALF
                block = ref[:, first : first + HALF].reshape(NZ * NY * HALF, ROWS)
                part = contract(block, weight[...], 1, 0)
                total = part if total is None else total + part
            out_ref[:, half * HALF : (half + 1) * HALF] = total.astype(jnp.bfloat16).reshape(
                NZ * NY, HALF, kvw
            )

    return call(kernel, shape((NZ * NY, TOK, kvw)), (own, other, *weights), flops=2**29)


def to_set(values):
    return lax.all_to_all(values, "dp", 0, 0, axis_index_groups=ZY_GROUPS)


def body(
    enc_states,
    kv_cotangent,
    out_cotangent,
    attn_context,
    next_states,
    next_context,
    kv_master,
    kv_first,
    kv_second,
    out_master,
    out_first,
    out_second,
):
    bf16, f32 = jnp.bfloat16, jnp.float32
    after = lax.optimization_barrier
    dp, tensor = lax.axis_index("dp"), lax.axis_index("tensor")
    x, z, y = dp // (NZ * NY), (dp // NY) % NZ, dp % NY
    h, core = tensor // NC, tensor % NC
    kv_scale = D ** (-0.5)
    out_scale = QD ** (-0.5)
    max_norm = clip_ratio * math.sqrt(D * (KVW + QD))
    kvw, qd = kv_cotangent.shape[1], attn_context.shape[1]
    place = jnp.stack([x, z, y, h, core]).astype(jnp.int32)
    kept_half = (core ^ z).astype(jnp.int32).reshape(1)

    out_sent = out_payload(place, out_cotangent, attn_context)
    out_landed = to_set(out_sent)
    place_kv, out_sent = after((place, out_sent))
    *kv_sent, kv_rest = kv_payload(place_kv, enc_states, kv_cotangent)
    kv_own = [kv_sent[0]] + [move_x(kv_sent[k], k) for k in range(1, NX)]
    context = swap_xh(next_context)
    kv_other = [kv_rest] + [move_core(part) for part in kv_own[1:]]

    kv_part = kv_terms(place, kv_own, kv_other, next_states, kvw, kv_scale)
    kv_part, out_landed, context = after((kv_part, out_landed, context))
    kv_landed = to_set(kv_part)
    out_other = move_core(out_landed[:, :, : 2 * ROWS])
    out_parts = out_terms(out_landed, out_other, qd, out_scale)
    context_z = move_z(context)
    out_parts = [out_parts[0]] + [move_x(out_parts[k], k) for k in range(1, NX)]
    out_grad, out_squares = sum_terms(out_parts, qd)
    kv_landed, out_squares, context_z = after((kv_landed, out_squares, context_z))
    context = jnp.stack([context, context_z])
    context = [context] + [move_h(context, j) for j in range(1, NH)]
    kv_grad, kv_squares = sum_terms([kv_landed], kvw)
    states_other = move_core(kv_landed[:, kvw:])

    n_all = NX * NZ * NY * NH * NC
    squares_all = lax.all_to_all(
        jnp.broadcast_to((kv_squares + out_squares).reshape(1, 1, 1), (n_all, 1, 128)),
        ("dp", "tensor"),
        0,
        0,
    )
    squares_all, context, states_other = after((squares_all, context, states_other))
    squares_total = jnp.sum(squares_all[:, 0, 0])
    factor = jnp.minimum(1.0, max_norm / (jnp.sqrt(squares_total) + 1e-06))
    new_out_master, new_out_first, new_out_second = adam_update(
        out_master, out_first, out_second, out_grad, factor
    )
    new_kv_master, new_kv_first, new_kv_second = adam_update(
        kv_master, kv_first, kv_second, kv_grad, factor
    )

    out_weight = swap_xh(new_out_master.astype(bf16))
    out_weight, kv_weight = after((out_weight, new_kv_master.astype(bf16)))
    out_weights = [out_weight] + [move_y(out_weight, j) for j in range(1, NY)]
    kv_weights = [kv_weight] + [move_x(kv_weight, j) for j in range(1, NX)]
    out_weights, kv_weights = after((out_weights, kv_weights))
    (sent,) = next_partial(place, 1 - kept_half, context, out_weights)
    arrived = move_core(sent)
    keyvalue = keyvalue_partial(kv_landed, states_other, kv_weights)
    arrived, keyvalue = after((arrived, keyvalue))
    kept = next_partial(place, kept_half, context, out_weights, arrived)
    homes = [move_home(block, k) for k, block in enumerate(kept)]
    homes[0], keyvalue = after((homes[0], keyvalue))
    next_output = sum(part.astype(f32) for part in homes).astype(bf16)

    keyvalue = to_set(keyvalue)
    keyvalue = jnp.sum(keyvalue.astype(f32), axis=0).astype(bf16)
    next_keyvalue = jnp.where(core == 0, keyvalue, jnp.roll(keyvalue, HALF, axis=0))
    return (
        new_kv_master,
        new_kv_first,
        new_kv_second,
        new_out_master,
        new_out_first,
        new_out_second,
        next_keyvalue,
        next_output,
    )


def solution(mesh):
    return jax.shard_map(
        body,
        mesh=mesh,
        in_specs=(
            P("dp", None),
            P("dp", "tensor"),
            P("dp", None),
            P("dp", "tensor"),
            P("dp", None),
            P("dp", "tensor"),
            P("dp", "tensor"),
            P("dp", "tensor"),
            P("dp", "tensor"),
            P("dp", "tensor"),
            P("dp", "tensor"),
            P("dp", "tensor"),
        ),
        out_specs=(
            P("dp", "tensor"),
            P("dp", "tensor"),
            P("dp", "tensor"),
            P("dp", "tensor"),
            P("dp", "tensor"),
            P("dp", "tensor"),
            P("dp", "tensor"),
            P("dp", "tensor"),
        ),
        check_vma=False,
    )
```

```python
import itertools
import math

import jax
import jax.numpy as jnp
from jax import lax
from jax.experimental import pallas as pl
from jax.experimental.pallas import tpu as pltpu
from jax.sharding import PartitionSpec as P

D = 8192
STEP = 10
KVW = 2048
QD = 4096

NX, NZ, NY = 4, 2, 4
NH, NC = 4, 2
TOK = 128
HALF = TOK // 2
ROWS = 256
WIDE = NX * ROWS

beta_one = 0.9
beta_two = 0.95
learn_rate = 0.01
weight_decay = 0.1
epsilon = 1e-08
clip_ratio = 0.25


def dp_of(x, z, y):
    return (x * NZ + z) * NY + y


ZY_GROUPS = [[dp_of(x, z, y) for z in range(NZ) for y in range(NY)] for x in range(NX)]


def device_pairs(target):
    pairs = []
    for x, z, y, h, c in itertools.product(
        range(NX), range(NZ), range(NY), range(NH), range(NC)
    ):
        tx, tz, ty, th, tc = target(x, z, y, h, c)
        source = (dp_of(x, z, y) * NH + h) * NC + c
        pairs.append((source, (dp_of(tx % NX, tz % NZ, ty % NY) * NH + th % NH) * NC + tc % NC))
    return pairs


def move(values, target):
    return lax.ppermute(values, ("dp", "tensor"), device_pairs(target))


def move_core(values):
    return move(values, lambda x, z, y, h, c: (x, z, y, h, c + 1))


def move_x(values, k):
    return move(values, lambda x, z, y, h, c: (x + k, z, y, h, c))


def move_y(values, k):
    return move(values, lambda x, z, y, h, c: (x, z, y + k, h, c))


def move_h(values, k):
    return move(values, lambda x, z, y, h, c: (x, z, y, h + k, c))


def move_z(values):
    return move(values, lambda x, z, y, h, c: (x, z + 1, y, h, c))


def move_home(values):
    return move(values, lambda x, z, y, h, c: (h, c, y, x, z))


def adam_update(master, first_moment, second_moment, gradient, factor):
    scaled = gradient * factor
    first_moment = beta_one * first_moment + (1.0 - beta_one) * scaled
    second_moment = beta_two * second_moment + (1.0 - beta_two) * scaled * scaled
    first_hat = first_moment / (1.0 - beta_one**STEP)
    second_hat = second_moment / (1.0 - beta_two**STEP)
    direction = first_hat / (jnp.sqrt(second_hat) + epsilon)
    master = master - learn_rate * (direction + weight_decay * master)
    return (master, first_moment, second_moment)


def dot(left, right, left_dims, right_dims):
    return lax.dot_general(
        left,
        right,
        ((left_dims, right_dims), ((), ())),
        preferred_element_type=jnp.float32,
    )


VMEM = pl.BlockSpec(memory_space=pltpu.VMEM)
SMEM = pl.BlockSpec(memory_space=pltpu.SMEM)


def call(kernel, out_shape, operands, scalars=(), flops=0, scratch=()):
    moved = sum(o.size * o.dtype.itemsize for o in (*operands, *jax.tree.leaves(out_shape)))
    return pl.pallas_call(
        kernel,
        out_shape=out_shape,
        in_specs=[SMEM] * len(scalars) + [VMEM] * len(operands),
        out_specs=jax.tree.map(lambda _: VMEM, out_shape),
        scratch_shapes=list(scratch),
        compiler_params=pltpu.CompilerParams(vmem_limit_bytes=40 * 2**20),
        cost_estimate=pl.CostEstimate(flops=flops, bytes_accessed=moved, transcendentals=0),
    )(*scalars, *operands)


def shape(dims, dtype=jnp.bfloat16):
    return jax.ShapeDtypeStruct(dims, dtype)


def contract(left, right, left_dim, right_dim):
    return lax.dot_general(
        left, right, (((left_dim,), (right_dim,)), ((), ())), preferred_element_type=jnp.float32
    )


def halves(core):
    own = pl.ds(pl.multiple_of(core * HALF, HALF), HALF)
    other = pl.ds(pl.multiple_of((1 - core) * HALF, HALF), HALF)
    return own, other


def columns_of(x, k, p=None):
    first = lax.rem(x + k, NX) * (NZ * NY)
    if p is None:
        return pl.ds(pl.multiple_of(first * ROWS, ROWS), NZ * NY * ROWS)
    return pl.ds(pl.multiple_of((first + p) * ROWS, ROWS), ROWS)


def kv_payload(place, enc_states, kv_cotangent):
    width = NZ * NY * ROWS
    kvw = kv_cotangent.shape[1]

    def kernel(place_ref, states_ref, cot_ref, o0, o1, o2, o3, rest_ref):
        x, core = place_ref[0], place_ref[4]
        own, other = halves(core)
        for k, out_ref in enumerate((o0, o1, o2, o3)):
            out_ref[:, :width] = states_ref[own, columns_of(x, k)]
            out_ref[:, width : width + kvw] = cot_ref[own, :]
            out_ref[:, width + kvw :] = cot_ref[other, :]
        rest_ref[...] = states_ref[other, columns_of(x, 0)]

    out_shape = (shape((HALF, width + 2 * kvw)),) * NX + (shape((HALF, width)),)
    return call(kernel, out_shape, (enc_states, kv_cotangent), (place,))


def out_payload(place, out_cotangent, attn_context):
    qd = attn_context.shape[1]

    def kernel(place_ref, cot_ref, context_ref, out_ref):
        x, core = place_ref[0], place_ref[4]
        own, other = halves(core)
        for p in range(NZ * NY):
            for k in range(NX):
                rows = slice((k // 2) * HALF, (k // 2 + 1) * HALF)
                cols = slice((k % 2) * ROWS, (k % 2 + 1) * ROWS)
                out_ref[p, rows, cols] = cot_ref[own, columns_of(x, k, p)]
            out_ref[p, :HALF, 2 * ROWS :] = context_ref[own, :]
            out_ref[p, HALF:, 2 * ROWS :] = context_ref[other, :]

    out_shape = shape((NZ * NY, TOK, 2 * ROWS + qd))
    return call(kernel, out_shape, (out_cotangent, attn_context), (place,))


def kv_terms(place, own, other, next_states, kvw, scale):
    width = NZ * NY * ROWS

    def kernel(place_ref, *refs):
        own_refs, other_refs, states_ref, out_ref = (
            refs[:NX],
            refs[NX : 2 * NX],
            refs[2 * NX],
            refs[2 * NX + 1],
        )
        x, core = place_ref[0], place_ref[4]
        half, _ = halves(core)
        own_cot = jnp.concatenate([r[:, width : width + kvw] for r in own_refs], axis=0)
        other_cot = jnp.concatenate([r[:, width + kvw :] for r in own_refs], axis=0)
        for p in range(NZ * NY):
            cols = slice(p * ROWS, (p + 1) * ROWS)
            term = contract(own_cot, jnp.concatenate([r[:, cols] for r in own_refs]), 0, 0)
            term += contract(other_cot, jnp.concatenate([r[:, cols] for r in other_refs]), 0, 0)
            out_ref[p, :kvw] = (term * scale).astype(jnp.bfloat16)
            for k in range(NX):
                rows = slice(kvw + k * HALF, kvw + (k + 1) * HALF)
                out_ref[p, rows] = states_ref[half, columns_of(x, k, p)]

    out_shape = shape((NZ * NY, kvw + NX * HALF, ROWS))
    return call(kernel, out_shape, (*own, *other, next_states), (place,), flops=2**29)


def out_terms(own, other, qd, scale):
    tokens = NZ * NY * HALF

    def kernel(own_ref, other_ref, *out_refs):
        own_context = own_ref[:, :HALF, 2 * ROWS :].reshape(tokens, qd)
        other_context = own_ref[:, HALF:, 2 * ROWS :].reshape(tokens, qd)
        for k, out_ref in enumerate(out_refs):
            rows = slice((k // 2) * HALF, (k // 2 + 1) * HALF)
            cols = slice((k % 2) * ROWS, (k % 2 + 1) * ROWS)
            term = contract(own_context, own_ref[:, rows, cols].reshape(tokens, ROWS), 0, 0)
            term += contract(other_context, other_ref[:, rows, cols].reshape(tokens, ROWS), 0, 0)
            out_ref[...] = (term * scale).astype(jnp.bfloat16)

    return call(kernel, (shape((qd, ROWS)),) * NX, (own, other), flops=2**30)


def sum_terms(terms, columns, squares=None, copies=None):
    rows = terms[0].shape[-1]

    def kernel(*refs):
        *refs, grad_ref, squares_ref = refs
        total = None
        for ref in refs[: len(terms)]:
            blocks = [ref[...]] if len(ref.shape) == 2 else [ref[i, :columns] for i in range(ref.shape[0])]
            for block in blocks:
                block = block.astype(jnp.float32)
                total = block if total is None else total + block
        if squares is None:
            squares_ref[0, 0] = jnp.sum(total * total)
        else:
            both = refs[-1][0, 0] + jnp.sum(total * total)
            squares_ref[...] = jnp.full(squares_ref.shape, both, jnp.float32)
        grad_ref[...] = total.T

    squares_shape = shape((1, 1) if squares is None else (copies, 1, 128), jnp.float32)
    return pl.pallas_call(
        kernel,
        out_shape=(shape((rows, columns), jnp.float32), squares_shape),
        in_specs=[VMEM] * len(terms) + [SMEM] * (squares is not None),
        out_specs=(VMEM, SMEM if squares is None else VMEM),
        compiler_params=pltpu.CompilerParams(vmem_limit_bytes=40 * 2**20),
        cost_estimate=pl.CostEstimate(flops=2**20, bytes_accessed=2**20, transcendentals=0),
    )(*terms, *([] if squares is None else [squares]))


def next_partial(place, which, context, context_z, weights, arrived=None):
    qd = context[0].shape[-1]
    n_in = NX + 1 + len(weights)

    def kernel(place_ref, which_ref, *refs):
        x, h = place_ref[0], place_ref[3]
        *refs, tokens_ref = refs
        outs = refs[n_in + (arrived is not None) :]

        def take(blocks):
            for j in range(NX):
                tokens_ref[lax.rem(x - j - h + 2 * NX, NX)] = blocks[j]

        @pl.when(which_ref[0] == 0)
        def _():
            take([ref[...] for ref in refs[:NX]])

        @pl.when(which_ref[0] != 0)
        def _():
            take([refs[NX][j] for j in range(NX)])

        tokens = tokens_ref[...].reshape(NX * TOK, qd)
        for j, weight_ref in enumerate(refs[NX + 1 : n_in]):
            cols = slice(j * ROWS, (j + 1) * ROWS)
            part = contract(tokens, weight_ref[...], 1, 1)
            if arrived is None:
                outs[0][:, cols] = part.astype(jnp.bfloat16)
            else:
                part += refs[n_in][:, cols].astype(jnp.float32)
                for k in range(NX):
                    outs[k][:, cols] = part[k * TOK : (k + 1) * TOK].astype(jnp.bfloat16)

    width = len(weights) * ROWS
    if arrived is None:
        out_shape = (shape((NX * TOK, width)),)
        operands = (*context, context_z, *weights)
    else:
        out_shape = (shape((TOK, width)),) * NX
        operands = (*context, context_z, *weights, arrived)
    scratch = [pltpu.VMEM((NX, TOK, qd), jnp.bfloat16)]
    return call(kernel, out_shape, operands, (place, which), 2**28, scratch)


def sum_homes(place, *chunks):
    def kernel(place_ref, *refs):
        *refs, out_ref = refs
        y, j = place_ref[2], 0
        for chunk in range(len(chunks)):
            total = None
            for ref in refs[chunk * NH : (chunk + 1) * NH]:
                part = ref[...].astype(jnp.float32)
                total = part if total is None else total + part
            for m in range(total.shape[1] // ROWS):
                cols = pl.ds(pl.multiple_of(lax.rem(y - j + NY, NY) * ROWS, ROWS), ROWS)
                out_ref[:, cols] = total[:, m * ROWS : (m + 1) * ROWS].astype(jnp.bfloat16)
                j += 1

    operands = [part for chunk in chunks for part in chunk]
    return call(kernel, shape((TOK, NY * ROWS)), operands, (place,))


def keyvalue_partial(place, own, other, weights):
    kvw = weights[0].shape[1]

    def kernel(place_ref, own_ref, other_ref, w0, w1, w2, w3, *out_refs):
        z, y = place_ref[1], place_ref[2]
        for q, out_ref in enumerate(out_refs):
            sets = [lax.rem(z + q, NZ) * NY + lax.rem(y + k, NY) for k in range(NY)]
            for half, ref in enumerate((own_ref, other_ref)):
                total = None
                for j, weight in enumerate((w0, w1, w2, w3)):
                    first = ref.shape[1] - (NX - -j % NX) * HALF
                    block = jnp.concatenate([ref[i, first : first + HALF] for i in sets], axis=0)
                    part = contract(block, weight[...], 1, 0)
                    total = part if total is None else total + part
                out_ref[:, half * HALF : (half + 1) * HALF] = total.astype(jnp.bfloat16).reshape(
                    NY, HALF, kvw
                )

    out_shape = (shape((NY, TOK, kvw)),) * NZ
    return call(kernel, out_shape, (own, other, *weights), (place,), 2**29)


def to_set(values):
    return lax.all_to_all(values, "dp", 0, 0, axis_index_groups=ZY_GROUPS)


def body(
    enc_states,
    kv_cotangent,
    out_cotangent,
    attn_context,
    next_states,
    next_context,
    kv_master,
    kv_first,
    kv_second,
    out_master,
    out_first,
    out_second,
):
    bf16, f32 = jnp.bfloat16, jnp.float32
    after = lax.optimization_barrier
    dp, tensor = lax.axis_index("dp"), lax.axis_index("tensor")
    x, z, y = dp // (NZ * NY), (dp // NY) % NZ, dp % NY
    h, core = tensor // NC, tensor % NC
    kv_scale = D ** (-0.5)
    out_scale = QD ** (-0.5)
    max_norm = clip_ratio * math.sqrt(D * (KVW + QD))
    kvw, qd = kv_cotangent.shape[1], attn_context.shape[1]
    place = jnp.stack([x, z, y, h, core]).astype(jnp.int32)
    kept_half = (core ^ z).astype(jnp.int32).reshape(1)

    out_sent = out_payload(place, out_cotangent, attn_context)
    out_landed = to_set(out_sent)
    place_kv, out_sent = after((place, out_sent))
    *kv_sent, kv_rest = kv_payload(place_kv, enc_states, kv_cotangent)
    kv_own = [kv_sent[0]] + [move_x(kv_sent[k], k) for k in range(1, NX)]
    kv_other = [kv_rest] + [move_core(part) for part in kv_own[1:]]

    kv_part = kv_terms(place, kv_own, kv_other, next_states, kvw, kv_scale)
    kv_part, out_landed = after((kv_part, out_landed))
    kv_landed = to_set(kv_part)
    out_other = move_core(out_landed[:, :, : 2 * ROWS])
    out_parts = out_terms(out_landed, out_other, qd, out_scale)
    context = [next_context] + [move_x(next_context, j) for j in range(1, NX)]
    out_parts = [out_parts[0]] + [move_x(out_parts[k], k) for k in range(1, NX)]
    out_grad, out_squares = sum_terms(out_parts, qd)
    kv_landed, out_squares = after((kv_landed, out_squares))
    n_all = NX * NZ * NY * NH * NC
    kv_grad, squares = sum_terms([kv_landed], kvw, out_squares, n_all)
    states_other = move_core(kv_landed)
    squares_all = lax.all_to_all(squares, ("dp", "tensor"), 0, 0)
    squares_all, context, states_other = after((squares_all, context, states_other))
    squares_total = jnp.sum(squares_all[:, 0, 0])
    factor = jnp.minimum(1.0, max_norm / (jnp.sqrt(squares_total) + 1e-06))
    new_out_master, new_out_first, new_out_second = adam_update(
        out_master, out_first, out_second, out_grad, factor
    )
    new_kv_master, new_kv_first, new_kv_second = adam_update(
        kv_master, kv_first, kv_second, kv_grad, factor
    )
    out_weight, kv_weight = new_out_master.astype(bf16), new_kv_master.astype(bf16)
    out_weights = [out_weight] + [move_y(out_weight, j) for j in range(1, NY)]
    kv_weights = [kv_weight] + [move_x(kv_weight, j) for j in range(1, NX)]
    out_weights, kv_weights = after((out_weights, kv_weights))
    context_z = move_z(jnp.stack(context))
    (sent,) = next_partial(place, 1 - kept_half, context, context_z, out_weights)
    arrived = move_core(sent)
    keyvalue = keyvalue_partial(place, kv_landed, states_other, kv_weights)
    arrived, keyvalue = after((arrived, keyvalue))
    kept = next_partial(place, kept_half, context, context_z, out_weights, arrived)
    parts = [kept[0]] + [move_h(kept[k], k) for k in range(1, NH)]
    next_output = move_home(sum_homes(place, parts))

    keyvalue = (keyvalue[0].astype(f32) + move_z(keyvalue[1]).astype(f32)).astype(bf16)
    keyvalue = [keyvalue[0]] + [move_y(keyvalue[k], k) for k in range(1, NY)]
    keyvalue = sum(part.astype(f32) for part in keyvalue).astype(bf16)
    next_keyvalue = jnp.where(core == 0, keyvalue, jnp.roll(keyvalue, HALF, axis=0))
    return (
        new_kv_master,
        new_kv_first,
        new_kv_second,
        new_out_master,
        new_out_first,
        new_out_second,
        next_keyvalue,
        next_output,
    )


def solution(mesh):
    return jax.shard_map(
        body,
        mesh=mesh,
        in_specs=(
            P("dp", None),
            P("dp", "tensor"),
            P("dp", None),
            P("dp", "tensor"),
            P("dp", None),
            P("dp", "tensor"),
            P("dp", "tensor"),
            P("dp", "tensor"),
            P("dp", "tensor"),
            P("dp", "tensor"),
            P("dp", "tensor"),
            P("dp", "tensor"),
        ),
        out_specs=(
            P("dp", "tensor"),
            P("dp", "tensor"),
            P("dp", "tensor"),
            P("dp", "tensor"),
            P("dp", "tensor"),
            P("dp", "tensor"),
            P("dp", "tensor"),
            P("dp", "tensor"),
        ),
        check_vma=False,
    )
```

```python
import itertools
import math

import jax
import jax.numpy as jnp
from jax import lax
from jax.experimental import pallas as pl
from jax.experimental.pallas import tpu as pltpu
from jax.sharding import PartitionSpec as P

D = 8192
STEP = 10
KVW = 2048
QD = 4096

NX, NZ, NY = 4, 2, 4
NH, NC = 4, 2
TOK = 128
HALF = TOK // 2
ROWS = 256
WIDE = NX * ROWS

beta_one = 0.9
beta_two = 0.95
learn_rate = 0.01
weight_decay = 0.1
epsilon = 1e-08
clip_ratio = 0.25


def dp_of(x, z, y):
    return (x * NZ + z) * NY + y


ZY_GROUPS = [[dp_of(x, z, y) for z in range(NZ) for y in range(NY)] for x in range(NX)]


def device_pairs(target):
    pairs = []
    for x, z, y, h, c in itertools.product(
        range(NX), range(NZ), range(NY), range(NH), range(NC)
    ):
        tx, tz, ty, th, tc = target(x, z, y, h, c)
        source = (dp_of(x, z, y) * NH + h) * NC + c
        pairs.append((source, (dp_of(tx % NX, tz % NZ, ty % NY) * NH + th % NH) * NC + tc % NC))
    return pairs


def move(values, target):
    return lax.ppermute(values, ("dp", "tensor"), device_pairs(target))


def move_core(values):
    return move(values, lambda x, z, y, h, c: (x, z, y, h, c + 1))


def move_x(values, k):
    return move(values, lambda x, z, y, h, c: (x + k, z, y, h, c))


def move_y(values, k):
    return move(values, lambda x, z, y, h, c: (x, z, y + k, h, c))


def move_h(values, k):
    return move(values, lambda x, z, y, h, c: (x, z, y, h + k, c))


def move_z(values):
    return move(values, lambda x, z, y, h, c: (x, z + 1, y, h, c))


def move_home(values):
    return move(values, lambda x, z, y, h, c: (h, c, y, x, z))


def adam_update(master, first_moment, second_moment, gradient, factor):
    scaled = gradient * factor
    first_moment = beta_one * first_moment + (1.0 - beta_one) * scaled
    second_moment = beta_two * second_moment + (1.0 - beta_two) * scaled * scaled
    first_hat = first_moment / (1.0 - beta_one**STEP)
    second_hat = second_moment / (1.0 - beta_two**STEP)
    direction = first_hat / (jnp.sqrt(second_hat) + epsilon)
    master = master - learn_rate * (direction + weight_decay * master)
    return (master, first_moment, second_moment)


def dot(left, right, left_dims, right_dims):
    return lax.dot_general(
        left,
        right,
        ((left_dims, right_dims), ((), ())),
        preferred_element_type=jnp.float32,
    )


VMEM = pl.BlockSpec(memory_space=pltpu.VMEM)
SMEM = pl.BlockSpec(memory_space=pltpu.SMEM)


def call(kernel, out_shape, operands, scalars=(), flops=0, scratch=()):
    moved = sum(o.size * o.dtype.itemsize for o in (*operands, *jax.tree.leaves(out_shape)))
    return pl.pallas_call(
        kernel,
        out_shape=out_shape,
        in_specs=[SMEM] * len(scalars) + [VMEM] * len(operands),
        out_specs=jax.tree.map(lambda _: VMEM, out_shape),
        scratch_shapes=list(scratch),
        compiler_params=pltpu.CompilerParams(vmem_limit_bytes=40 * 2**20),
        cost_estimate=pl.CostEstimate(flops=flops, bytes_accessed=moved, transcendentals=0),
    )(*scalars, *operands)


def shape(dims, dtype=jnp.bfloat16):
    return jax.ShapeDtypeStruct(dims, dtype)


def contract(left, right, left_dim, right_dim):
    return lax.dot_general(
        left, right, (((left_dim,), (right_dim,)), ((), ())), preferred_element_type=jnp.float32
    )


def halves(core):
    own = pl.ds(pl.multiple_of(core * HALF, HALF), HALF)
    other = pl.ds(pl.multiple_of((1 - core) * HALF, HALF), HALF)
    return own, other


def columns_of(x, k, p=None):
    first = lax.rem(x + k, NX) * (NZ * NY)
    if p is None:
        return pl.ds(pl.multiple_of(first * ROWS, ROWS), NZ * NY * ROWS)
    return pl.ds(pl.multiple_of((first + p) * ROWS, ROWS), ROWS)


def kv_payload(place, enc_states, kv_cotangent):
    width = NZ * NY * ROWS
    kvw = kv_cotangent.shape[1]

    def kernel(place_ref, states_ref, cot_ref, o0, o1, o2, o3, rest_ref):
        x, core = place_ref[0], place_ref[4]
        own, other = halves(core)
        for k, out_ref in enumerate((o0, o1, o2, o3)):
            out_ref[:, :width] = states_ref[own, columns_of(x, k)]
            out_ref[:, width : width + kvw] = cot_ref[own, :]
            out_ref[:, width + kvw :] = cot_ref[other, :]
        rest_ref[...] = states_ref[other, columns_of(x, 0)]

    out_shape = (shape((HALF, width + 2 * kvw)),) * NX + (shape((HALF, width)),)
    return call(kernel, out_shape, (enc_states, kv_cotangent), (place,))


def out_payload(place, out_cotangent, attn_context):
    qd = attn_context.shape[1]

    def kernel(place_ref, cot_ref, context_ref, out_ref):
        x, core = place_ref[0], place_ref[4]
        own, other = halves(core)
        for p in range(NZ * NY):
            for k in range(NX):
                rows = slice((k // 2) * HALF, (k // 2 + 1) * HALF)
                cols = slice((k % 2) * ROWS, (k % 2 + 1) * ROWS)
                out_ref[p, rows, cols] = cot_ref[own, columns_of(x, k, p)]
            out_ref[p, :HALF, 2 * ROWS :] = context_ref[own, :]
            out_ref[p, HALF:, 2 * ROWS :] = context_ref[other, :]

    out_shape = shape((NZ * NY, TOK, 2 * ROWS + qd))
    return call(kernel, out_shape, (out_cotangent, attn_context), (place,))


def kv_terms(place, own, other, next_states, kvw, scale):
    width = NZ * NY * ROWS

    def kernel(place_ref, *refs):
        own_refs, other_refs, states_ref, out_ref = (
            refs[:NX],
            refs[NX : 2 * NX],
            refs[2 * NX],
            refs[2 * NX + 1],
        )
        x, core = place_ref[0], place_ref[4]
        half, _ = halves(core)
        own_cot = jnp.concatenate([r[:, width : width + kvw] for r in own_refs], axis=0)
        other_cot = jnp.concatenate([r[:, width + kvw :] for r in own_refs], axis=0)
        for p in range(NZ * NY):
            cols = slice(p * ROWS, (p + 1) * ROWS)
            term = contract(own_cot, jnp.concatenate([r[:, cols] for r in own_refs]), 0, 0)
            term += contract(other_cot, jnp.concatenate([r[:, cols] for r in other_refs]), 0, 0)
            out_ref[p, :kvw] = (term * scale).astype(jnp.bfloat16)
            for k in range(NX):
                rows = slice(kvw + k * HALF, kvw + (k + 1) * HALF)
                out_ref[p, rows] = states_ref[half, columns_of(x, k, p)]

    out_shape = shape((NZ * NY, kvw + NX * HALF, ROWS))
    return call(kernel, out_shape, (*own, *other, next_states), (place,), flops=2**29)


def out_terms(own, other, qd, scale):
    tokens = NZ * NY * HALF

    def kernel(own_ref, other_ref, *out_refs):
        own_context = own_ref[:, :HALF, 2 * ROWS :].reshape(tokens, qd)
        other_context = own_ref[:, HALF:, 2 * ROWS :].reshape(tokens, qd)
        for k, out_ref in enumerate(out_refs):
            rows = slice((k // 2) * HALF, (k // 2 + 1) * HALF)
            cols = slice((k % 2) * ROWS, (k % 2 + 1) * ROWS)
            term = contract(own_context, own_ref[:, rows, cols].reshape(tokens, ROWS), 0, 0)
            term += contract(other_context, other_ref[:, rows, cols].reshape(tokens, ROWS), 0, 0)
            out_ref[...] = (term * scale).astype(jnp.bfloat16)

    return call(kernel, (shape((qd, ROWS)),) * NX, (own, other), flops=2**30)


def sum_terms(terms, columns, squares=None, copies=None):
    rows = terms[0].shape[-1]

    def kernel(*refs):
        *refs, grad_ref, squares_ref = refs
        total = None
        for ref in refs[: len(terms)]:
            blocks = [ref[...]] if len(ref.shape) == 2 else [ref[i, :columns] for i in range(ref.shape[0])]
            for block in blocks:
                block = block.astype(jnp.float32)
                total = block if total is None else total + block
        if squares is None:
            squares_ref[0, 0] = jnp.sum(total * total)
        else:
            both = refs[-1][0, 0] + jnp.sum(total * total)
            squares_ref[...] = jnp.full(squares_ref.shape, both, jnp.float32)
        grad_ref[...] = total.T

    squares_shape = shape((1, 1) if squares is None else (copies, 1, 128), jnp.float32)
    return pl.pallas_call(
        kernel,
        out_shape=(shape((rows, columns), jnp.float32), squares_shape),
        in_specs=[VMEM] * len(terms) + [SMEM] * (squares is not None),
        out_specs=(VMEM, SMEM if squares is None else VMEM),
        compiler_params=pltpu.CompilerParams(vmem_limit_bytes=40 * 2**20),
        cost_estimate=pl.CostEstimate(flops=2**20, bytes_accessed=2**20, transcendentals=0),
    )(*terms, *([] if squares is None else [squares]))


def next_partial(place, which, context, context_z, weights, arrived=None):
    qd = context[0].shape[-1]
    n_in = NX + 1 + len(weights)

    def kernel(place_ref, which_ref, *refs):
        x, h = place_ref[0], place_ref[3]
        *refs, tokens_ref = refs
        outs = refs[n_in + (arrived is not None) :]

        def take(blocks):
            for j in range(NX):
                tokens_ref[lax.rem(x - j - h + 2 * NX, NX)] = blocks[j]

        @pl.when(which_ref[0] == 0)
        def _():
            take([ref[...] for ref in refs[:NX]])

        @pl.when(which_ref[0] != 0)
        def _():
            take([refs[NX][j] for j in range(NX)])

        tokens = tokens_ref[...].reshape(NX * TOK, qd)
        for j, weight_ref in enumerate(refs[NX + 1 : n_in]):
            cols = slice(j * ROWS, (j + 1) * ROWS)
            part = contract(tokens, weight_ref[...], 1, 1)
            if arrived is None:
                outs[0][:, cols] = part.astype(jnp.bfloat16)
            else:
                part += refs[n_in][:, cols].astype(jnp.float32)
                for k in range(NX):
                    outs[k][:, cols] = part[k * TOK : (k + 1) * TOK].astype(jnp.bfloat16)

    width = len(weights) * ROWS
    if arrived is None:
        out_shape = (shape((NX * TOK, width)),)
        operands = (*context, context_z, *weights)
    else:
        out_shape = (shape((TOK, width)),) * NX
        operands = (*context, context_z, *weights, arrived)
    scratch = [pltpu.VMEM((NX, TOK, qd), jnp.bfloat16)]
    return call(kernel, out_shape, operands, (place, which), 2**28, scratch)


def sum_homes(place, *chunks):
    def kernel(place_ref, *refs):
        *refs, out_ref = refs
        y, j = place_ref[2], 0
        for chunk in range(len(chunks)):
            total = None
            for ref in refs[chunk * NH : (chunk + 1) * NH]:
                part = ref[...].astype(jnp.float32)
                total = part if total is None else total + part
            for m in range(total.shape[1] // ROWS):
                cols = pl.ds(pl.multiple_of(lax.rem(y - j + NY, NY) * ROWS, ROWS), ROWS)
                out_ref[:, cols] = total[:, m * ROWS : (m + 1) * ROWS].astype(jnp.bfloat16)
                j += 1

    operands = [part for chunk in chunks for part in chunk]
    return call(kernel, shape((TOK, NY * ROWS)), operands, (place,))


def keyvalue_partial(place, own, other, weights):
    kvw = weights[0].shape[1]

    def kernel(place_ref, own_ref, other_ref, w0, w1, w2, w3, *out_refs):
        z, y = place_ref[1], place_ref[2]
        for q, out_ref in enumerate(out_refs):
            sets = [lax.rem(z + q, NZ) * NY + lax.rem(y + k, NY) for k in range(NY)]
            for half, ref in enumerate((own_ref, other_ref)):
                total = None
                for j, weight in enumerate((w0, w1, w2, w3)):
                    first = ref.shape[1] - (NX - -j % NX) * HALF
                    block = jnp.concatenate([ref[i, first : first + HALF] for i in sets], axis=0)
                    part = contract(block, weight[...], 1, 0)
                    total = part if total is None else total + part
                out_ref[:, half * HALF : (half + 1) * HALF] = total.astype(jnp.bfloat16).reshape(
                    NY, HALF, kvw
                )

    out_shape = (shape((NY, TOK, kvw)),) * NZ
    return call(kernel, out_shape, (own, other, *weights), (place,), 2**29)


def to_set(values):
    return lax.all_to_all(values, "dp", 0, 0, axis_index_groups=ZY_GROUPS)


def body(
    enc_states,
    kv_cotangent,
    out_cotangent,
    attn_context,
    next_states,
    next_context,
    kv_master,
    kv_first,
    kv_second,
    out_master,
    out_first,
    out_second,
):
    bf16, f32 = jnp.bfloat16, jnp.float32
    after = lax.optimization_barrier
    dp, tensor = lax.axis_index("dp"), lax.axis_index("tensor")
    x, z, y = dp // (NZ * NY), (dp // NY) % NZ, dp % NY
    h, core = tensor // NC, tensor % NC
    kv_scale = D ** (-0.5)
    out_scale = QD ** (-0.5)
    max_norm = clip_ratio * math.sqrt(D * (KVW + QD))
    kvw, qd = kv_cotangent.shape[1], attn_context.shape[1]
    place = jnp.stack([x, z, y, h, core]).astype(jnp.int32)
    kept_half = (core ^ z).astype(jnp.int32).reshape(1)

    out_sent = out_payload(place, out_cotangent, attn_context)
    out_landed = to_set(out_sent)
    place_kv, out_sent = after((place, out_sent))
    *kv_sent, kv_rest = kv_payload(place_kv, enc_states, kv_cotangent)
    kv_own = [kv_sent[0]] + [move_x(kv_sent[k], k) for k in range(1, NX)]
    kv_other = [kv_rest] + [move_core(part) for part in kv_own[1:]]

    kv_part = kv_terms(place, kv_own, kv_other, next_states, kvw, kv_scale)
    kv_part, out_landed = after((kv_part, out_landed))
    kv_landed = to_set(kv_part)
    out_other = move_core(out_landed[:, :, : 2 * ROWS])
    out_parts = out_terms(out_landed, out_other, qd, out_scale)
    context = [next_context] + [move_x(next_context, j) for j in range(1, NX)]
    out_parts = [out_parts[0]] + [move_x(out_parts[k], k) for k in range(1, NX)]
    out_grad, out_squares = sum_terms(out_parts, qd)
    kv_landed, out_squares = after((kv_landed, out_squares))
    n_all = NX * NZ * NY * NH * NC
    kv_grad, squares = sum_terms([kv_landed], kvw, out_squares, n_all)
    states_other = move_core(kv_landed)
    squares_all = lax.all_to_all(squares, ("dp", "tensor"), 0, 0)
    squares_all, context, states_other = after((squares_all, context, states_other))
    squares_total = jnp.sum(squares_all[:, 0, 0])
    factor = jnp.minimum(1.0, max_norm / (jnp.sqrt(squares_total) + 1e-06))
    out_weight = adam_update(out_master, out_first, out_second, out_grad, factor)[0].astype(bf16)
    new_kv_master, new_kv_first, new_kv_second = adam_update(
        kv_master, kv_first, kv_second, kv_grad, factor
    )
    kv_weight = new_kv_master.astype(bf16)
    out_weights = [out_weight] + [move_y(out_weight, j) for j in range(1, NY)]
    kv_weights = [kv_weight] + [move_x(kv_weight, j) for j in range(1, NX)]
    out_weights, kv_weights = after((out_weights, kv_weights))
    context_z = move_z(jnp.stack(context))
    (sent,) = next_partial(place, 1 - kept_half, context, context_z, out_weights)
    arrived = move_core(sent)
    keyvalue = keyvalue_partial(place, kv_landed, states_other, kv_weights)
    arrived, keyvalue = after((arrived, keyvalue))
    kept = next_partial(place, kept_half, context, context_z, out_weights, arrived)
    parts = [kept[0]] + [move_h(kept[k], k) for k in range(1, NH)]
    next_output = move_home(sum_homes(place, parts))
    out_grad, factor, _ = after((out_grad, factor, kept[0]))
    new_out_master, new_out_first, new_out_second = adam_update(
        out_master, out_first, out_second, out_grad, factor
    )

    keyvalue = (keyvalue[0].astype(f32) + move_z(keyvalue[1]).astype(f32)).astype(bf16)
    keyvalue = [keyvalue[0]] + [move_y(keyvalue[k], k) for k in range(1, NY)]
    keyvalue = sum(part.astype(f32) for part in keyvalue).astype(bf16)
    next_keyvalue = jnp.where(core == 0, keyvalue, jnp.roll(keyvalue, HALF, axis=0))
    return (
        new_kv_master,
        new_kv_first,
        new_kv_second,
        new_out_master,
        new_out_first,
        new_out_second,
        next_keyvalue,
        next_output,
    )


def solution(mesh):
    return jax.shard_map(
        body,
        mesh=mesh,
        in_specs=(
            P("dp", None),
            P("dp", "tensor"),
            P("dp", None),
            P("dp", "tensor"),
            P("dp", None),
            P("dp", "tensor"),
            P("dp", "tensor"),
            P("dp", "tensor"),
            P("dp", "tensor"),
            P("dp", "tensor"),
            P("dp", "tensor"),
            P("dp", "tensor"),
        ),
        out_specs=(
            P("dp", "tensor"),
            P("dp", "tensor"),
            P("dp", "tensor"),
            P("dp", "tensor"),
            P("dp", "tensor"),
            P("dp", "tensor"),
            P("dp", "tensor"),
            P("dp", "tensor"),
        ),
        check_vma=False,
    )
```
